32 devices in a mesh: group: 8 (over z, y), head: 4 (over x, core).
Axes of the slice: x: 2, y: 2, z: 4, core: 2. Of those that a mesh axis runs over, the one named last changes fastest.
Arguments:
- queries: bfloat16 [2048, 3072], P('group', 'head'), may hold values from -160 to 160, as said below
- keys_new: bfloat16 [2048, 3072], P('group', 'head'), may hold values from -7 to 7, as said below
- values_new: bfloat16 [2048, 3072], P('group', 'head'), may hold values from -6 to 6
- cache_keys: bfloat16 [512, 3072], P('group', 'head'), may hold values from -6 to 6
- cache_values: bfloat16 [512, 3072], P('group', 'head'), may hold values from -6 to 6
- valid_rows: int32 [8], replicated, may hold values from 32 to 64
- finished: int32 [8], replicated, may hold values from 5 to 8
- levels: int32 [8], P('group'), may hold values from 0 to 63
- gate_table: float32 [64, 6144], P(None, 'head'), may hold values from 0.5 to 4
- out_weight: bfloat16 [3072, 6144], P(None, 'head'), may hold values from -1.75 to 1.75
- latents: bfloat16 [48, 256, 512], P('group', 'head'), may hold values from -6 to 6
- conv_weight: bfloat16 [3, 512, 512], replicated, may hold values from -0.15625 to 0.15625
Outputs:
- mixed: bfloat16 [2048, 6144], P('group', 'head')
- decoded: bfloat16 [48, 256, 512], P('group', 'head')
The draws below stay inside these ranges and needn't reach their ends.
Inputs may be any that keep to these rules, and one draw needn't show every extreme that they name: `queries`: normal entries, with some rows made large multiples of keys in some draws. `keys_new`: normal entries.
All inputs are finite; a program needn't handle non-finite values.
Results may differ from the reference program's by a relative error of at most 0.01.
Values may be sent and summed in bfloat16 or wider, within the bound.
A program may use at most 128 MiB of HBM per device.

```python
import math
import jax
import jax.numpy as jnp
from jax import lax

D = 6144
HEADS = 24
HD = 128
QROWS = 256
KROWS = 64
NLEV = 64
FR = 6
CH = 512
GROUPS = 8
PIX = 256
N_GROUP = 8


def shared_keys(key):
    rows_total = GROUPS * QROWS
    base = jnp.clip(jax.random.normal(jax.random.fold_in(key, 101), (rows_total, HEADS * HD), jnp.float32), -6.0, 6.0)
    nudge = 0.1 * jnp.clip(jax.random.normal(jax.random.fold_in(key, 102), (rows_total, HEADS * HD), jnp.float32), -6.0, 6.0)
    position = jnp.arange(rows_total) % QROWS
    follow = jnp.roll(base, 1, axis=0) + nudge
    return jnp.where((position == 9)[:, None], follow, base)


def draw_keys_new(key, part):
    return shared_keys(key).astype(jnp.bfloat16)


def draw_queries(key, part):
    key = jax.random.fold_in(key, 7)
    rows_total = GROUPS * QROWS
    drawn = jnp.clip(jax.random.normal(key, (rows_total, HEADS * HD), jnp.float32), -6.0, 6.0)
    return drawn.astype(jnp.bfloat16)


def set_ends(entries, stream_key, low, top_value):
    longest = entries.shape.index(max(entries.shape))
    spots = []
    for shift in (0, 1):
        where = [jax.random.randint(jax.random.fold_in(stream_key, axis), (), 0, length) for axis, length in enumerate(entries.shape)]
        where[longest] = (where[longest] + shift) % entries.shape[longest]
        spots.append(tuple(where))
    return entries.at[spots[0]].set(low).at[spots[1]].set(top_value)


def steps_of(key, shape, cuts, least, high):
    def one(dim, parts):
        draws = jax.random.uniform(jax.random.fold_in(jax.random.fold_in(key, 6), dim), (parts,), jnp.float32, least / len(cuts), high / len(cuts))
        return jnp.repeat(jnp.exp(draws), shape[dim] // parts).reshape((-1,) + (1,) * (len(shape) - dim - 1))

    factor_of = one(*cuts[0])
    for cut in cuts[1:]:
        factor_of = factor_of * one(*cut)
    return factor_of


def centred(key, extent, width, bound, pieces=(), kind=jnp.bfloat16):
    entries = width * jax.random.normal(key, extent, jnp.float32)
    if pieces:
        entries = entries * steps_of(key, extent, pieces, -0.22, 0.18)
    return jnp.clip(entries, -bound, bound).astype(kind)


def setup_inputs(seed: int = 0) -> dict:
    seeds = jax.random.split(jax.random.key(seed), 13)
    return {
        "queries": draw_queries(jax.random.fold_in(seeds[12], 71), 0),
        "keys_new": draw_keys_new(jax.random.fold_in(seeds[12], 71), 0),
        "values_new": centred(seeds[2], (GROUPS * QROWS, HEADS * HD), 1.0, 6.0, ((0, 8), (1, 4))),
        "cache_keys": centred(seeds[3], (GROUPS * KROWS, HEADS * HD), 1.0, 6.0, ((0, 8), (1, 4))),
        "cache_values": centred(seeds[4], (GROUPS * KROWS, HEADS * HD), 1.0, 6.0, ((0, 8), (1, 4))),
        "valid_rows": set_ends(jax.random.randint(seeds[5], (GROUPS,), KROWS // 2, KROWS + 1), jax.random.fold_in(seeds[5], 1), KROWS // 2, KROWS).astype(jnp.int32),
        "finished": set_ends(jax.random.randint(seeds[6], (GROUPS,), N_GROUP // 2 + 1, N_GROUP + 1), jax.random.fold_in(seeds[6], 1), N_GROUP // 2 + 1, N_GROUP).astype(jnp.int32),
        "levels": set_ends(jax.random.randint(seeds[7], (GROUPS,), 0, NLEV), jax.random.fold_in(seeds[7], 1), 0, NLEV - 1).astype(jnp.int32),
        "gate_table": jnp.clip(jnp.exp(math.log(4.0) - 2.0794415 * jax.random.uniform(seeds[8], (NLEV, D), jnp.float32) ** steps_of(seeds[8], (NLEV, D), ((1, 4),), -0.2, 0.2)), 0.5, 4.0),
        "out_weight": centred(seeds[9], (HEADS * HD, D), (max(1, (HEADS * HD) // 256)) ** -0.5, 1.75, ((1, 4),)),
        "latents": centred(seeds[10], (GROUPS * FR, PIX, CH), 1.0, 6.0, ((0, 8), (1, 4))),
        "conv_weight": centred(seeds[11], (3, CH, CH), (3 * CH) ** -0.5, 0.15625),
    }


def reference(queries, keys_new, values_new, cache_keys, cache_values, valid_rows, finished, levels, gate_table, out_weight, latents, conv_weight):
    scale_factor = HD ** -0.5
    cached_k = cache_keys.reshape(GROUPS * KROWS, HEADS, HD).astype(jnp.float32)
    cached_v = cache_values.reshape(GROUPS * KROWS, HEADS, HD).astype(jnp.float32)
    rows_all = jnp.arange(GROUPS * KROWS, dtype=jnp.int32)
    owner = rows_all // KROWS
    offset = rows_all % KROWS
    own_ones = jnp.ones((QROWS,), dtype=bool)

    def one_group(index):
        first = (index * QROWS).astype(jnp.int32)
        usable = (owner < finished[index]) & (offset < valid_rows[owner])
        usable_all = jnp.concatenate([own_ones, usable])
        query_rows = lax.dynamic_slice_in_dim(queries, first, QROWS, 0).reshape(QROWS, HEADS, HD).astype(jnp.float32)
        own_k = lax.dynamic_slice_in_dim(keys_new, first, QROWS, 0).reshape(QROWS, HEADS, HD).astype(jnp.float32)
        own_v = lax.dynamic_slice_in_dim(values_new, first, QROWS, 0).reshape(QROWS, HEADS, HD).astype(jnp.float32)
        every_k = jnp.concatenate([own_k, cached_k], axis=0)
        every_v = jnp.concatenate([own_v, cached_v], axis=0)
        scores = jnp.einsum('qhd,khd->hqk', query_rows, every_k) * scale_factor
        scores = jnp.where(usable_all[None, None, :], scores, -jnp.inf)
        topmost = jnp.max(scores, axis=-1, keepdims=True)
        weights = jnp.where(usable_all[None, None, :], jnp.exp(scores - topmost), 0.0)
        totals = jnp.sum(weights, axis=-1)
        rounded = weights.astype(jnp.bfloat16).astype(jnp.float32)
        summed = jnp.einsum('hqk,khd->hqd', rounded, every_v)
        result = summed / totals[..., None]
        return jnp.transpose(result, (1, 0, 2)).reshape(QROWS, HEADS * HD).astype(jnp.bfloat16)

    attended = lax.map(one_group, jnp.arange(GROUPS, dtype=jnp.int32)).reshape(GROUPS * QROWS, HEADS * HD)
    projected = jnp.dot(attended, out_weight, preferred_element_type=jnp.float32)
    gates = jnp.repeat(gate_table[levels], QROWS, axis=0)
    mixed = (projected * gates).astype(jnp.bfloat16)

    frames_total = GROUPS * FR
    padded = jnp.concatenate([jnp.zeros((2, PIX, CH), dtype=latents.dtype), latents], axis=0).astype(jnp.float32)
    taps = conv_weight.astype(jnp.float32)
    decoded = jnp.zeros((frames_total, PIX, CH), dtype=jnp.float32)
    for k in range(3):
        decoded = decoded + jnp.einsum('tpc,cd->tpd', padded[2 - k:2 - k + frames_total], taps[k])
    return mixed, decoded.astype(jnp.bfloat16)
```

```python
import functools

import jax
import jax.numpy as jnp
from jax import lax
from jax.experimental import pallas as pl
from jax.experimental.pallas import tpu as pltpu
from jax.sharding import PartitionSpec as P

HD = 128
NEGATIVE = -1e30
LOG2E = 1.4426950408889634
MESH = pl.DeviceIdType.MESH
NT = (((1,), (1,)), ((), ()))


def kernel(
    cfg,
    q_hbm, kn_hbm, vn_hbm, ck_hbm, cv_hbm,
    valid_ref, finished_ref, level_ref,
    gate_hbm, w_hbm, lat_hbm, cw_hbm,
    mixed_ref, dec_ref,
    kv, q, kn, vn, att, w, gate, ext, cw, acc, bias,
    kv_load, w_load, load, kv_recv, up_send, down_send, y_send,
    att_recv, att_send, halo_send, halo_recv,
):
    groups, pieces, per, ahead, crossing = cfg
    lines = groups // 2
    krows = kv.shape[4]
    heads_local = pieces * per
    n_head = att.shape[1]
    wide = per * HD
    pix = ext.shape[0] - lat_hbm.shape[0]
    rows = lat_hbm.shape[0]

    g = lax.axis_index("group")
    hd = lax.axis_index("head")
    z, y = g // 2, g % 2
    has_up, has_down = z < lines - 1, z > 0
    y_peer = z * 2 + 1 - y
    core_peer = (hd // 2) * 2 + 1 - hd % 2
    x_peer = (hd + 2) % n_head

    kv_copies = []
    for h in range(heads_local):
        for i, src in enumerate((ck_hbm, cv_hbm)):
            kv_copies.append(pltpu.make_async_copy(
                src.at[:, pl.ds(h * HD, HD)], kv.at[h // per, g, h % per, i], kv_load.at[2 * h + i]))
    for c in kv_copies:
        c.start()
    lat_copy = pltpu.make_async_copy(lat_hbm, ext.at[pl.ds(pix, rows)], load.at[0])
    cw_copy = pltpu.make_async_copy(cw_hbm, cw, load.at[1])
    q_copy = pltpu.make_async_copy(q_hbm, q, load.at[2])
    kn_copy = pltpu.make_async_copy(kn_hbm, kn, load.at[3])
    vn_copy = pltpu.make_async_copy(vn_hbm, vn, load.at[4])
    gate_copy = pltpu.make_async_copy(gate_hbm, gate, load.at[5])
    for c in (lat_copy, cw_copy, q_copy, kn_copy, vn_copy):
        c.start()

    barrier = pltpu.get_barrier_semaphore()

    def greet(group, head):
        pl.semaphore_signal(barrier, inc=1, device_id={"group": group, "head": head}, device_id_type=MESH)

    greet(y_peer, hd)
    greet(g, core_peer)
    greet(g, x_peer)
    diag = jnp.where(y == 0, g - 1, g + 1)
    has_diag = jnp.where(y == 0, has_down, has_up)

    @pl.when(has_up)
    def _():
        greet(g + 2, hd)

    @pl.when(has_down)
    def _():
        greet(g - 2, hd)

    @pl.when(has_diag)
    def _():
        greet(diag, hd)

    pl.semaphore_wait(
        barrier, 3 + has_up.astype(jnp.int32) + has_down.astype(jnp.int32) + has_diag.astype(jnp.int32))

    def send_up(p, s):
        return pltpu.make_async_remote_copy(
            kv.at[p, s], kv.at[p, s], up_send.at[p, s], kv_recv.at[p, s],
            device_id={"group": g + 2, "head": hd}, device_id_type=MESH)

    def send_down(p, s):
        return pltpu.make_async_remote_copy(
            kv.at[p, s], kv.at[p, s], down_send.at[p, s], kv_recv.at[p, s],
            device_id={"group": g - 2, "head": hd}, device_id_type=MESH)

    def send_y(p, s):
        return pltpu.make_async_remote_copy(
            kv.at[p, s], kv.at[p, s], y_send.at[p, s // 2], kv_recv.at[p, s],
            device_id={"group": y_peer, "head": hd}, device_id_type=MESH)

    def received(p, s):
        send_y(p, s).wait_recv()

    def both_ways(p, s):
        @pl.when(has_up)
        def _():
            send_up(p, s).start()

        @pl.when(has_down)
        def _():
            send_down(p, s).start()

    def own_sends(p):
        for h in range(p * per, p * per + per):
            kv_copies[2 * h].wait()
            kv_copies[2 * h + 1].wait()
        if p in crossing:
            send_y(p, g).start()
            both_ways(p, g)
        else:
            both_ways(p, g)
            send_y(p, g).start()

    def forward(p):
        cross = p in crossing
        columns = (y, 1 - y) if cross else (y,)
        if cross:
            received(p, y_peer)
            both_ways(p, y_peer)

        def step(t, _):
            for col in columns:
                @pl.when(z >= t)
                def _():
                    s = (z - t) * 2 + col
                    received(p, s)

                    @pl.when(has_up)
                    def _():
                        send_up(p, s).start()

                    if not cross:
                        send_y(p, s).start()

                @pl.when(z + t < lines)
                def _():
                    s = (z + t) * 2 + col
                    received(p, s)

                    @pl.when(has_down)
                    def _():
                        send_down(p, s).start()

                    if not cross:
                        send_y(p, s).start()
            return 0

        lax.fori_loop(1, lines, step, 0)
        if not cross:
            def side(s, _):
                received(p, s * 2 + 1 - y)
                return 0

            lax.fori_loop(0, lines, side, 0)

    def finish_sends(p):
        cross = p in crossing

        def one(s, _):
            for col in ((0, 1) if cross else (y,)):
                @pl.when(has_up & (s <= z))
                def _():
                    send_up(p, s * 2 + col).wait_send()

                @pl.when(has_down & (s >= z))
                def _():
                    send_down(p, s * 2 + col).wait_send()
            if not cross:
                send_y(p, s * 2 + y).wait_send()
            return 0

        lax.fori_loop(0, lines, one, 0)
        if cross:
            send_y(p, g).wait_send()

    def att_copy(p, slot, which, peer):
        return pltpu.make_async_remote_copy(
            att.at[p, slot], att.at[p, slot], att_send.at[p, which], att_recv.at[p, slot],
            device_id={"group": g, "head": peer}, device_id_type=MESH)

    def attend(p):
        block_groups = min(groups, 8)
        width = block_groups * krows
        for j in range(per):
            h = p * per + j
            cols = pl.ds(h * HD, HD)
            qh = q[:, cols]

            def cached(b, i):
                return kv[p, b * block_groups:(b + 1) * block_groups, j, i].reshape(width, HD)

            def scores(b):
                s = lax.dot_general(qh, cached(b, 0), NT, preferred_element_type=jnp.float32)
                return s * (HD ** -0.5 * LOG2E) + bias[:, b * width:(b + 1) * width]

            own = lax.dot_general(qh, kn[:, cols], NT, preferred_element_type=jnp.float32) * (HD ** -0.5 * LOG2E)
            first = scores(0)
            top = jnp.maximum(jnp.max(own, axis=1, keepdims=True), jnp.max(first, axis=1, keepdims=True))
            w_own = jnp.exp2(own - top)
            w_first = jnp.exp2(first - top)
            total = jnp.sum(w_own, axis=1, keepdims=True) + jnp.sum(w_first, axis=1, keepdims=True)
            summed = jnp.dot(w_own.astype(jnp.bfloat16), vn[:, cols], preferred_element_type=jnp.float32)
            summed += jnp.dot(w_first.astype(jnp.bfloat16), cached(0, 1), preferred_element_type=jnp.float32)
            for b in range(1, groups // block_groups):
                s = scores(b)
                new = jnp.maximum(top, jnp.max(s, axis=1, keepdims=True))
                rescale = jnp.exp2(top - new)
                wb = jnp.exp2(s - new)
                total = total * rescale + jnp.sum(wb, axis=1, keepdims=True)
                summed = summed * rescale + jnp.dot(
                    wb.astype(jnp.bfloat16), cached(b, 1), preferred_element_type=jnp.float32)
                top = new
            att[p, hd, :, pl.ds(j * HD, HD)] = (summed / total).astype(jnp.bfloat16)
        att_copy(p, hd, 1, x_peer).start()
        att_copy(p, hd, 0, core_peer).start()

    def relay(p):
        att_copy(p, x_peer, 2, core_peer).wait_recv()
        att_copy(p, x_peer, 2, core_peer).start()

    def project(p):
        other = (core_peer + 2) % n_head
        att_copy(p, core_peer, 0, core_peer).wait_recv()
        att_copy(p, other, 0, core_peer).wait_recv()
        for c in w_copies[p]:
            c.wait()
        rows_in = jnp.concatenate([att[p, i] for i in range(n_head)], axis=1)
        tile = 512
        for n in range(0, acc.shape[1], tile):
            part = jnp.dot(rows_in, w[p, :, n:n + tile], preferred_element_type=jnp.float32)
            if p > 0:
                part = part + acc[:, n:n + tile]
            if p < pieces - 1:
                acc[:, n:n + tile] = part
            else:
                row = gate[pl.ds(level_ref[0], 1), n:n + tile]
                mixed_ref[:, n:n + tile] = (part * row).astype(jnp.bfloat16)

    def convolve(first, number):
        at = [ext[pix + first - k * (pix // 2): pix + first - k * (pix // 2) + number, :] for k in range(3)]
        total = jnp.dot(at[0], cw[0], preferred_element_type=jnp.float32)
        total += jnp.dot(at[1], cw[1], preferred_element_type=jnp.float32)
        total += jnp.dot(at[2], cw[2], preferred_element_type=jnp.float32)
        dec_ref[first:first + number, :] = total.astype(jnp.bfloat16)

    halo = pltpu.make_async_remote_copy(
        ext.at[pl.ds(rows, pix)], ext.at[pl.ds(0, pix)], halo_send, halo_recv,
        device_id={"group": g + 1, "head": hd}, device_id_type=MESH)

    for p in range(min(ahead, pieces)):
        own_sends(p)

    w_copies = []
    for p in range(pieces):
        w_copies.append([
            pltpu.make_async_copy(
                w_hbm.at[pl.ds((i * heads_local + p * per) * HD, wide)],
                w.at[p, pl.ds(i * wide, wide)], w_load.at[p, i])
            for i in range(n_head)])
        for c in w_copies[-1]:
            c.start()
    gate_copy.start()

    position = lax.broadcasted_iota(jnp.int32, (1, groups * krows), 1)
    owner, offset = position // krows, position % krows
    limit = jnp.zeros((1, groups * krows), jnp.int32)
    for j in range(groups):
        limit = jnp.where(owner == j, valid_ref[j], limit)
    usable = (owner < finished_ref[g]) & (offset < limit)
    bias[...] = jnp.where(usable, 0.0, NEGATIVE)

    @pl.when(g == 0)
    def _():
        ext[0:pix, :] = jnp.zeros((pix, ext.shape[1]), ext.dtype)

    lat_copy.wait()
    cw_copy.wait()
    convolve(pix, rows - pix)
    q_copy.wait()
    kn_copy.wait()
    vn_copy.wait()

    for p in range(pieces):
        if p + ahead < pieces:
            own_sends(p + ahead)
        forward(p)
        if p == pieces - 1:
            @pl.when(g < groups - 1)
            def _():
                halo.start()
        attend(p)
        if p >= 1:
            relay(p - 1)
        if p >= 2:
            project(p - 2)

    gate_copy.wait()
    if pieces >= 2:
        project(pieces - 2)

    @pl.when(g > 0)
    def _():
        halo.wait_recv()

    relay(pieces - 1)
    convolve(0, pix)
    project(pieces - 1)

    @pl.when(g < groups - 1)
    def _():
        halo.wait_send()

    for p in range(pieces):
        finish_sends(p)
        att_copy(p, hd, 1, x_peer).wait_send()
        att_copy(p, hd, 0, core_peer).wait_send()
        att_copy(p, x_peer, 2, core_peer).wait_send()


def shards(
    groups, n_head,
    queries, keys_new, values_new, cache_keys, cache_values,
    valid_rows, finished, levels, gate_table, out_weight, latents, conv_weight,
):
    qrows, width = queries.shape
    krows = cache_keys.shape[0]
    heads_local = width // HD
    features = out_weight.shape[1]
    frames, pixels, channels = latents.shape
    pieces = heads_local if groups <= 8 else 1
    per = heads_local // pieces
    crossing = (0,) if pieces > 1 else ()
    cfg = (groups, pieces, per, 2, crossing)
    lines = groups // 2
    bf16, f32 = jnp.bfloat16, jnp.float32
    dma = pltpu.SemaphoreType.DMA
    hbm = pl.BlockSpec(memory_space=pl.ANY)
    smem = pl.BlockSpec(memory_space=pltpu.SMEM)
    vmem = pl.BlockSpec(memory_space=pltpu.VMEM)
    mixed, decoded = pl.pallas_call(
        functools.partial(kernel, cfg),
        out_shape=(
            jax.ShapeDtypeStruct((qrows, features), bf16),
            jax.ShapeDtypeStruct((frames * pixels, channels), bf16),
        ),
        in_specs=[hbm] * 5 + [smem] * 3 + [hbm] * 4,
        out_specs=(vmem, vmem),
        scratch_shapes=[
            pltpu.VMEM((pieces, groups, per, 2, krows, HD), bf16),
            pltpu.VMEM((qrows, width), bf16),
            pltpu.VMEM((qrows, width), bf16),
            pltpu.VMEM((qrows, width), bf16),
            pltpu.VMEM((pieces, n_head, qrows, per * HD), bf16),
            pltpu.VMEM((pieces, n_head * per * HD, features), bf16),
            pltpu.VMEM(gate_table.shape, f32),
            pltpu.VMEM(((frames + 2) * pixels, channels), bf16),
            pltpu.VMEM(conv_weight.shape, bf16),
            pltpu.VMEM((qrows, features), f32),
            pltpu.VMEM((1, groups * krows), f32),
            dma((2 * heads_local,)),
            dma((pieces, n_head)),
            dma((6,)),
            dma((pieces, groups)),
            dma((pieces, groups)),
            dma((pieces, groups)),
            dma((pieces, lines)),
            dma((pieces, n_head)),
            dma((pieces, 3)),
            dma,
            dma,
        ],
        compiler_params=pltpu.CompilerParams(
            collective_id=0, has_side_effects=True, vmem_limit_bytes=56 * 2**20),
        name="video_attention",
    )(
        queries, keys_new, values_new, cache_keys, cache_values,
        valid_rows, finished, levels, gate_table, out_weight,
        latents.reshape(frames * pixels, channels), conv_weight,
    )
    return mixed, decoded.reshape(frames, pixels, channels)


def solution(mesh):
    in_specs = (
        P("group", "head"),
        P("group", "head"),
        P("group", "head"),
        P("group", "head"),
        P("group", "head"),
        P(),
        P(),
        P("group"),
        P(None, "head"),
        P(None, "head"),
        P("group", "head", None),
        P(),
    )
    out_specs = (P("group", "head"), P("group", "head", None))
    body = functools.partial(shards, mesh.shape["group"], mesh.shape["head"])
    return jax.shard_map(body, mesh=mesh, in_specs=in_specs, out_specs=out_specs, check_vma=False)
```

```python
import functools

import jax
import jax.numpy as jnp
from jax import lax
from jax.experimental import pallas as pl
from jax.experimental.pallas import tpu as pltpu
from jax.sharding import PartitionSpec as P

HD = 128
NEGATIVE = -1e30
LOG2E = 1.4426950408889634
MESH = pl.DeviceIdType.MESH
NT = (((1,), (1,)), ((), ()))


def kernel(
    cfg,
    q_hbm, kn_hbm, vn_hbm, ck_hbm, cv_hbm,
    valid_ref, finished_ref, level_ref,
    gate_hbm, w_hbm, lat_hbm, cw_hbm,
    mixed_ref, dec_ref,
    kv, q, kn, vn, att, w, gate, ext, cw, acc, bias,
    kv_load, w_load, load, kv_recv, up_send, down_send, y_send,
    att_recv, att_send, halo_send, halo_recv,
):
    groups, pieces, per, ahead, skew, reach, crossing = cfg
    lines = groups // 2
    krows = kv.shape[4]
    heads_local = pieces * per
    n_head = att.shape[1]
    wide = per * HD
    pix = ext.shape[0] - lat_hbm.shape[0]
    rows = lat_hbm.shape[0]

    g = lax.axis_index("group")
    hd = lax.axis_index("head")
    z, y = g // 2, g % 2
    has_up, has_down = z < lines - 1, z > 0
    y_peer = z * 2 + 1 - y
    core_peer = (hd // 2) * 2 + 1 - hd % 2
    x_peer = (hd + 2) % n_head

    kv_copies = []
    for h in range(heads_local):
        for i, src in enumerate((ck_hbm, cv_hbm)):
            kv_copies.append(pltpu.make_async_copy(
                src.at[:, pl.ds(h * HD, HD)], kv.at[h // per, g, h % per, i], kv_load.at[2 * h + i]))
    for c in kv_copies:
        c.start()
    lat_copy = pltpu.make_async_copy(lat_hbm, ext.at[pl.ds(pix, rows)], load.at[0])
    cw_copy = pltpu.make_async_copy(cw_hbm, cw, load.at[1])
    q_copy = pltpu.make_async_copy(q_hbm, q, load.at[2])
    kn_copy = pltpu.make_async_copy(kn_hbm, kn, load.at[3])
    vn_copy = pltpu.make_async_copy(vn_hbm, vn, load.at[4])
    gate_copy = pltpu.make_async_copy(gate_hbm, gate, load.at[5])
    for c in (lat_copy, cw_copy, q_copy, kn_copy, vn_copy):
        c.start()

    barrier = pltpu.get_barrier_semaphore()

    def greet(group, head):
        pl.semaphore_signal(barrier, inc=1, device_id={"group": group, "head": head}, device_id_type=MESH)

    greet(y_peer, hd)
    greet(g, core_peer)
    greet(g, x_peer)
    diag = jnp.where(y == 0, g - 1, g + 1)
    has_diag = jnp.where(y == 0, has_down, has_up)

    met = 3 + has_diag.astype(jnp.int32)
    for r in range(1, reach + 1):
        met += (z + r < lines).astype(jnp.int32) + (z >= r).astype(jnp.int32)

        @pl.when(z + r < lines)
        def _():
            greet(g + 2 * r, hd)

        @pl.when(z >= r)
        def _():
            greet(g - 2 * r, hd)

    @pl.when(has_diag)
    def _():
        greet(diag, hd)

    pl.semaphore_wait(barrier, met)

    def send_up(p, s, r):
        return pltpu.make_async_remote_copy(
            kv.at[p, s], kv.at[p, s], up_send.at[p, s, r - 1], kv_recv.at[p, s],
            device_id={"group": g + 2 * r, "head": hd}, device_id_type=MESH)

    def send_down(p, s, r):
        return pltpu.make_async_remote_copy(
            kv.at[p, s], kv.at[p, s], down_send.at[p, s, r - 1], kv_recv.at[p, s],
            device_id={"group": g - 2 * r, "head": hd}, device_id_type=MESH)

    def send_y(p, s):
        return pltpu.make_async_remote_copy(
            kv.at[p, s], kv.at[p, s], y_send.at[p, s // 2], kv_recv.at[p, s],
            device_id={"group": y_peer, "head": hd}, device_id_type=MESH)

    def received(p, s):
        send_y(p, s).wait_recv()

    def all_up(p, s, start):
        for r in range(reach, 0, -1):
            @pl.when(z + r < lines)
            def _():
                copy = send_up(p, s, r)
                copy.start() if start else copy.wait_send()

    def all_down(p, s, start):
        for r in range(reach, 0, -1):
            @pl.when(z >= r)
            def _():
                copy = send_down(p, s, r)
                copy.start() if start else copy.wait_send()

    def both_ways(p, s):
        all_up(p, s, True)
        all_down(p, s, True)

    def loaded(p):
        for h in range(p * per, p * per + per):
            kv_copies[2 * h].wait()
            kv_copies[2 * h + 1].wait()

    def own_sends(p):
        if p in crossing:
            both_ways(p, g)
        else:
            loaded(p)
            both_ways(p, g)
            send_y(p, g).start()

    def pass_on(p, t, col, cross):
        @pl.when(z >= t)
        def _():
            s = (z - t) * 2 + col
            received(p, s)
            if t % reach == 0:
                all_up(p, s, True)

            if not cross:
                send_y(p, s).start()

        @pl.when(z + t < lines)
        def _():
            s = (z + t) * 2 + col
            received(p, s)
            if t % reach == 0:
                all_down(p, s, True)

            if not cross:
                send_y(p, s).start()

    last = -(-(lines - 1) // reach) + 1

    def forward(k):
        for p in range(pieces):
            hop, rest = divmod(k - p, skew)
            cross = p in crossing
            if rest or hop < 1 or hop > last:
                continue
            near = range((hop - 1) * reach + 1, min(hop * reach, lines - 1) + 1)
            far = range((hop - 2) * reach + 1, min((hop - 1) * reach, lines - 1) + 1)
            if cross and hop == 1:
                received(p, y_peer)
                both_ways(p, y_peer)
            for t in near:
                pass_on(p, t, y, cross)
            if cross and hop > 1:
                for t in far:
                    pass_on(p, t, 1 - y, cross)
            if not cross and hop == last:
                def side(s, _):
                    received(p, s * 2 + 1 - y)
                    return 0

                lax.fori_loop(0, lines, side, 0)

    def finish_sends(p):
        cross = p in crossing
        for t in range(0, lines, reach):
            for col in ((0, 1) if cross else (y,)):
                @pl.when(z >= t)
                def _():
                    all_up(p, (z - t) * 2 + col, False)

                @pl.when(z + t < lines)
                def _():
                    all_down(p, (z + t) * 2 + col, False)
        if cross:
            send_y(p, g).wait_send()
        else:
            def one(s, _):
                send_y(p, s * 2 + y).wait_send()
                return 0

            lax.fori_loop(0, lines, one, 0)

    def att_copy(p, slot, which, peer):
        return pltpu.make_async_remote_copy(
            att.at[p, slot], att.at[p, slot], att_send.at[p, which], att_recv.at[p, slot],
            device_id={"group": g, "head": peer}, device_id_type=MESH)

    def attend(p):
        block_groups = min(groups, 8)
        width = block_groups * krows
        for j in range(per):
            h = p * per + j
            cols = pl.ds(h * HD, HD)
            qh = q[:, cols]

            def cached(b, i):
                return kv[p, b * block_groups:(b + 1) * block_groups, j, i].reshape(width, HD)

            def scores(b):
                s = lax.dot_general(qh, cached(b, 0), NT, preferred_element_type=jnp.float32)
                return s * (HD ** -0.5 * LOG2E) + bias[:, b * width:(b + 1) * width]

            own = lax.dot_general(qh, kn[:, cols], NT, preferred_element_type=jnp.float32) * (HD ** -0.5 * LOG2E)
            first = scores(0)
            top = jnp.maximum(jnp.max(own, axis=1, keepdims=True), jnp.max(first, axis=1, keepdims=True))
            w_own = jnp.exp2(own - top)
            w_first = jnp.exp2(first - top)
            total = jnp.sum(w_own, axis=1, keepdims=True) + jnp.sum(w_first, axis=1, keepdims=True)
            summed = jnp.dot(w_own.astype(jnp.bfloat16), vn[:, cols], preferred_element_type=jnp.float32)
            summed += jnp.dot(w_first.astype(jnp.bfloat16), cached(0, 1), preferred_element_type=jnp.float32)
            for b in range(1, groups // block_groups):
                s = scores(b)
                new = jnp.maximum(top, jnp.max(s, axis=1, keepdims=True))
                rescale = jnp.exp2(top - new)
                wb = jnp.exp2(s - new)
                total = total * rescale + jnp.sum(wb, axis=1, keepdims=True)
                summed = summed * rescale + jnp.dot(
                    wb.astype(jnp.bfloat16), cached(b, 1), preferred_element_type=jnp.float32)
                top = new
            att[p, hd, :, pl.ds(j * HD, HD)] = (summed / total).astype(jnp.bfloat16)
        att_copy(p, hd, 1, x_peer).start()
        att_copy(p, hd, 0, core_peer).start()

    def relay(p):
        att_copy(p, x_peer, 2, core_peer).wait_recv()
        att_copy(p, x_peer, 2, core_peer).start()

    def project(p):
        other = (core_peer + 2) % n_head
        att_copy(p, core_peer, 0, core_peer).wait_recv()
        att_copy(p, other, 0, core_peer).wait_recv()
        for c in w_copies[p]:
            c.wait()
        rows_in = jnp.concatenate([att[p, i] for i in range(n_head)], axis=1)
        tile = 512
        for n in range(0, acc.shape[1], tile):
            part = jnp.dot(rows_in, w[p, :, n:n + tile], preferred_element_type=jnp.float32)
            if p > 0:
                part = part + acc[:, n:n + tile]
            if p < pieces - 1:
                acc[:, n:n + tile] = part
            else:
                row = gate[pl.ds(level_ref[0], 1), n:n + tile]
                mixed_ref[:, n:n + tile] = (part * row).astype(jnp.bfloat16)

    def convolve(first, number):
        at = [ext[pix + first - k * (pix // 2): pix + first - k * (pix // 2) + number, :] for k in range(3)]
        total = jnp.dot(at[0], cw[0], preferred_element_type=jnp.float32)
        total += jnp.dot(at[1], cw[1], preferred_element_type=jnp.float32)
        total += jnp.dot(at[2], cw[2], preferred_element_type=jnp.float32)
        dec_ref[first:first + number, :] = total.astype(jnp.bfloat16)

    halo = pltpu.make_async_remote_copy(
        ext.at[pl.ds(rows, pix)], ext.at[pl.ds(0, pix)], halo_send, halo_recv,
        device_id={"group": g + 1, "head": hd}, device_id_type=MESH)

    for p in range(min(ahead, pieces)):
        own_sends(p)
    for p in crossing:
        loaded(p)
        send_y(p, g).start()

    w_copies = []
    for p in range(pieces):
        w_copies.append([
            pltpu.make_async_copy(
                w_hbm.at[pl.ds((i * heads_local + p * per) * HD, wide)],
                w.at[p, pl.ds(i * wide, wide)], w_load.at[p, i])
            for i in range(n_head)])
        for c in w_copies[-1]:
            c.start()
    gate_copy.start()

    position = lax.broadcasted_iota(jnp.int32, (1, groups * krows), 1)
    owner, offset = position // krows, position % krows
    limit = jnp.zeros((1, groups * krows), jnp.int32)
    for j in range(groups):
        limit = jnp.where(owner == j, valid_ref[j], limit)
    usable = (owner < finished_ref[g]) & (offset < limit)
    bias[...] = jnp.where(usable, 0.0, NEGATIVE)

    @pl.when(g == 0)
    def _():
        ext[0:pix, :] = jnp.zeros((pix, ext.shape[1]), ext.dtype)

    lat_copy.wait()
    cw_copy.wait()
    convolve(pix, rows - pix)
    q_copy.wait()
    kn_copy.wait()
    vn_copy.wait()

    for k in range(pieces + skew * last):
        forward(k)
        if ahead <= k - skew + ahead < pieces:
            own_sends(k - skew + ahead)
        p = k - skew * last
        if p == pieces - 1:
            @pl.when(g < groups - 1)
            def _():
                halo.start()
        if p >= 0:
            attend(p)
        if p >= 1:
            relay(p - 1)
        if p >= 2:
            project(p - 2)

    gate_copy.wait()
    if pieces >= 2:
        project(pieces - 2)

    relay(pieces - 1)

    @pl.when(g > 0)
    def _():
        halo.wait_recv()

    convolve(0, pix)
    project(pieces - 1)

    @pl.when(g < groups - 1)
    def _():
        halo.wait_send()

    for p in range(pieces):
        finish_sends(p)
        att_copy(p, hd, 1, x_peer).wait_send()
        att_copy(p, hd, 0, core_peer).wait_send()
        att_copy(p, x_peer, 2, core_peer).wait_send()


def hand_over_kernel(mixed, decoded, mixed_out, decoded_out, sems):
    copies = [
        pltpu.make_async_copy(mixed, mixed_out, sems.at[0]),
        pltpu.make_async_copy(decoded, decoded_out, sems.at[1]),
    ]
    for c in copies:
        c.start()
    for c in copies:
        c.wait()


def hand_over(mixed, decoded):
    anywhere = pl.BlockSpec(memory_space=pl.ANY)
    vmem = pl.BlockSpec(memory_space=pltpu.VMEM)
    return pl.pallas_call(
        hand_over_kernel,
        out_shape=(
            jax.ShapeDtypeStruct(mixed.shape, mixed.dtype),
            jax.ShapeDtypeStruct(decoded.shape, decoded.dtype),
        ),
        in_specs=[vmem, vmem],
        out_specs=(anywhere, anywhere),
        scratch_shapes=[pltpu.SemaphoreType.DMA((2,))],
        name="hand_over",
    )(mixed, decoded)


def shards(
    groups, n_head,
    queries, keys_new, values_new, cache_keys, cache_values,
    valid_rows, finished, levels, gate_table, out_weight, latents, conv_weight,
):
    qrows, width = queries.shape
    krows = cache_keys.shape[0]
    heads_local = width // HD
    features = out_weight.shape[1]
    frames, pixels, channels = latents.shape
    pieces = heads_local if groups <= 8 else 1
    reach = min(1, groups // 2 - 1)
    per = heads_local // pieces
    crossing = ()
    cfg = (groups, pieces, per, 3, 2, reach, crossing)
    lines = groups // 2
    bf16, f32 = jnp.bfloat16, jnp.float32
    dma = pltpu.SemaphoreType.DMA
    hbm = pl.BlockSpec(memory_space=pl.ANY)
    smem = pl.BlockSpec(memory_space=pltpu.SMEM)
    vmem = pl.BlockSpec(memory_space=pltpu.VMEM)
    mixed, decoded = pl.pallas_call(
        functools.partial(kernel, cfg),
        out_shape=(
            jax.ShapeDtypeStruct((qrows, features), bf16),
            jax.ShapeDtypeStruct((frames * pixels, channels), bf16),
        ),
        in_specs=[hbm] * 5 + [smem] * 3 + [hbm] * 4,
        out_specs=(vmem, vmem),
        scratch_shapes=[
            pltpu.VMEM((pieces, groups, per, 2, krows, HD), bf16),
            pltpu.VMEM((qrows, width), bf16),
            pltpu.VMEM((qrows, width), bf16),
            pltpu.VMEM((qrows, width), bf16),
            pltpu.VMEM((pieces, n_head, qrows, per * HD), bf16),
            pltpu.VMEM((pieces, n_head * per * HD, features), bf16),
            pltpu.VMEM(gate_table.shape, f32),
            pltpu.VMEM(((frames + 2) * pixels, channels), bf16),
            pltpu.VMEM(conv_weight.shape, bf16),
            pltpu.VMEM((qrows, features), f32),
            pltpu.VMEM((1, groups * krows), f32),
            dma((2 * heads_local,)),
            dma((pieces, n_head)),
            dma((6,)),
            dma((pieces, groups)),
            dma((pieces, groups, reach)),
            dma((pieces, groups, reach)),
            dma((pieces, lines)),
            dma((pieces, n_head)),
            dma((pieces, 3)),
            dma,
            dma,
        ],
        compiler_params=pltpu.CompilerParams(
            collective_id=0, has_side_effects=True, vmem_limit_bytes=56 * 2**20),
        name="video_attention",
    )(
        queries, keys_new, values_new, cache_keys, cache_values,
        valid_rows, finished, levels, gate_table, out_weight,
        latents.reshape(frames * pixels, channels), conv_weight,
    )
    mixed, decoded = hand_over(mixed, decoded)
    return mixed, decoded.reshape(frames, pixels, channels)


def solution(mesh):
    in_specs = (
        P("group", "head"),
        P("group", "head"),
        P("group", "head"),
        P("group", "head"),
        P("group", "head"),
        P(),
        P(),
        P("group"),
        P(None, "head"),
        P(None, "head"),
        P("group", "head", None),
        P(),
    )
    out_specs = (P("group", "head"), P("group", "head", None))
    body = functools.partial(shards, mesh.shape["group"], mesh.shape["head"])
    return jax.shard_map(body, mesh=mesh, in_specs=in_specs, out_specs=out_specs, check_vma=False)
```

```python
import functools

import jax
import jax.numpy as jnp
from jax import lax
from jax.experimental import pallas as pl
from jax.experimental.pallas import tpu as pltpu
from jax.sharding import PartitionSpec as P

HD = 128
NEGATIVE = -1e30
LOG2E = 1.4426950408889634
MESH = pl.DeviceIdType.MESH
NT = (((1,), (1,)), ((), ()))


def kernel(
    cfg,
    q_hbm, kn_hbm, vn_hbm, ck_hbm, cv_hbm,
    valid_ref, finished_ref, level_ref,
    gate_hbm, w_hbm, lat_hbm, cw_hbm,
    mixed_ref, dec_ref,
    kv, q, kn, vn, att, w, gate, ext, cw, acc, bias,
    kv_load, w_load, load, kv_recv, up_send, down_send, y_send,
    att_recv, att_send, halo_send, halo_recv,
):
    groups, pieces, per, ahead, skew, reach, crossing = cfg
    lines = groups // 2
    krows = kv.shape[4]
    heads_local = pieces * per
    n_head = att.shape[1]
    wide = per * HD
    pix = ext.shape[0] - lat_hbm.shape[0]
    rows = lat_hbm.shape[0]

    g = lax.axis_index("group")
    hd = lax.axis_index("head")
    z, y = g // 2, g % 2
    has_up, has_down = z < lines - 1, z > 0
    y_peer = z * 2 + 1 - y
    core_peer = (hd // 2) * 2 + 1 - hd % 2
    x_peer = (hd + 2) % n_head

    kv_copies = []
    for h in range(heads_local):
        for i, src in enumerate((ck_hbm, cv_hbm)):
            kv_copies.append(pltpu.make_async_copy(
                src.at[:, pl.ds(h * HD, HD)], kv.at[h // per, g, h % per, i], kv_load.at[2 * h + i]))
    for c in kv_copies:
        c.start()
    lat_copy = pltpu.make_async_copy(lat_hbm, ext.at[pl.ds(pix, rows)], load.at[0])
    cw_copy = pltpu.make_async_copy(cw_hbm, cw, load.at[1])
    q_copy = pltpu.make_async_copy(q_hbm, q, load.at[2])
    kn_copy = pltpu.make_async_copy(kn_hbm, kn, load.at[3])
    vn_copy = pltpu.make_async_copy(vn_hbm, vn, load.at[4])
    gate_copy = pltpu.make_async_copy(gate_hbm, gate, load.at[5])
    for c in (lat_copy, cw_copy, q_copy, kn_copy, vn_copy):
        c.start()

    barrier = pltpu.get_barrier_semaphore()

    def greet(group, head):
        pl.semaphore_signal(barrier, inc=1, device_id={"group": group, "head": head}, device_id_type=MESH)

    greet(y_peer, hd)
    greet(g, core_peer)
    greet(g, x_peer)
    diag = jnp.where(y == 0, g - 1, g + 1)
    has_diag = jnp.where(y == 0, has_down, has_up)

    met = 3 + has_diag.astype(jnp.int32)
    for r in range(1, reach + 1):
        met += (z + r < lines).astype(jnp.int32) + (z >= r).astype(jnp.int32)

        @pl.when(z + r < lines)
        def _():
            greet(g + 2 * r, hd)

        @pl.when(z >= r)
        def _():
            greet(g - 2 * r, hd)

    @pl.when(has_diag)
    def _():
        greet(diag, hd)

    pl.semaphore_wait(barrier, met)

    def send_up(p, s, r):
        return pltpu.make_async_remote_copy(
            kv.at[p, s], kv.at[p, s], up_send.at[p, s, r - 1], kv_recv.at[p, s],
            device_id={"group": g + 2 * r, "head": hd}, device_id_type=MESH)

    def send_down(p, s, r):
        return pltpu.make_async_remote_copy(
            kv.at[p, s], kv.at[p, s], down_send.at[p, s, r - 1], kv_recv.at[p, s],
            device_id={"group": g - 2 * r, "head": hd}, device_id_type=MESH)

    def send_y(p, s):
        return pltpu.make_async_remote_copy(
            kv.at[p, s], kv.at[p, s], y_send.at[p, s // 2], kv_recv.at[p, s],
            device_id={"group": y_peer, "head": hd}, device_id_type=MESH)

    def received(p, s):
        send_y(p, s).wait_recv()

    def all_up(p, s, start):
        for r in range(reach, 0, -1):
            @pl.when(z + r < lines)
            def _():
                copy = send_up(p, s, r)
                copy.start() if start else copy.wait_send()

    def all_down(p, s, start):
        for r in range(reach, 0, -1):
            @pl.when(z >= r)
            def _():
                copy = send_down(p, s, r)
                copy.start() if start else copy.wait_send()

    def both_ways(p, s):
        all_up(p, s, True)
        all_down(p, s, True)

    def loaded(p):
        for h in range(p * per, p * per + per):
            kv_copies[2 * h].wait()
            kv_copies[2 * h + 1].wait()

    def own_sends(p):
        if p in crossing:
            both_ways(p, g)
        else:
            loaded(p)
            both_ways(p, g)
            send_y(p, g).start()

    def pass_on(p, t, col, cross):
        @pl.when(z >= t)
        def _():
            s = (z - t) * 2 + col
            received(p, s)
            if t % reach == 0:
                all_up(p, s, True)

            if not cross:
                send_y(p, s).start()

        @pl.when(z + t < lines)
        def _():
            s = (z + t) * 2 + col
            received(p, s)
            if t % reach == 0:
                all_down(p, s, True)

            if not cross:
                send_y(p, s).start()

    last = -(-(lines - 1) // reach) + 1

    def forward(k):
        for p in range(pieces):
            hop, rest = divmod(k - p, skew)
            cross = p in crossing
            if rest or hop < 1 or hop > last:
                continue
            near = range((hop - 1) * reach + 1, min(hop * reach, lines - 1) + 1)
            far = range((hop - 2) * reach + 1, min((hop - 1) * reach, lines - 1) + 1)
            if cross and hop == 1:
                received(p, y_peer)
                both_ways(p, y_peer)
            for t in near:
                pass_on(p, t, y, cross)
            if cross and hop > 1:
                for t in far:
                    pass_on(p, t, 1 - y, cross)
            if not cross and hop == last:
                def side(s, _):
                    received(p, s * 2 + 1 - y)
                    return 0

                lax.fori_loop(0, lines, side, 0)

    def finish_sends(p):
        cross = p in crossing
        for t in range(0, lines, reach):
            for col in ((0, 1) if cross else (y,)):
                @pl.when(z >= t)
                def _():
                    all_up(p, (z - t) * 2 + col, False)

                @pl.when(z + t < lines)
                def _():
                    all_down(p, (z + t) * 2 + col, False)
        if cross:
            send_y(p, g).wait_send()
        else:
            def one(s, _):
                send_y(p, s * 2 + y).wait_send()
                return 0

            lax.fori_loop(0, lines, one, 0)

    def att_copy(p, slot, which, peer):
        return pltpu.make_async_remote_copy(
            att.at[p, slot], att.at[p, slot], att_send.at[p, which], att_recv.at[p, slot],
            device_id={"group": g, "head": peer}, device_id_type=MESH)

    def attend(p):
        block_groups = min(groups, 8)
        width = block_groups * krows
        for j in range(per):
            h = p * per + j
            cols = pl.ds(h * HD, HD)
            qh = q[:, cols]

            def cached(b, i):
                return kv[p, b * block_groups:(b + 1) * block_groups, j, i].reshape(width, HD)

            def scores(b):
                s = lax.dot_general(qh, cached(b, 0), NT, preferred_element_type=jnp.float32)
                return s * (HD ** -0.5 * LOG2E) + bias[:, b * width:(b + 1) * width]

            own = lax.dot_general(qh, kn[:, cols], NT, preferred_element_type=jnp.float32) * (HD ** -0.5 * LOG2E)
            first = scores(0)
            top = jnp.maximum(jnp.max(own, axis=1, keepdims=True), jnp.max(first, axis=1, keepdims=True))
            w_own = jnp.exp2(own - top)
            w_first = jnp.exp2(first - top)
            total = jnp.sum(w_own, axis=1, keepdims=True) + jnp.sum(w_first, axis=1, keepdims=True)
            summed = jnp.dot(w_own.astype(jnp.bfloat16), vn[:, cols], preferred_element_type=jnp.float32)
            summed += jnp.dot(w_first.astype(jnp.bfloat16), cached(0, 1), preferred_element_type=jnp.float32)
            for b in range(1, groups // block_groups):
                s = scores(b)
                new = jnp.maximum(top, jnp.max(s, axis=1, keepdims=True))
                rescale = jnp.exp2(top - new)
                wb = jnp.exp2(s - new)
                total = total * rescale + jnp.sum(wb, axis=1, keepdims=True)
                summed = summed * rescale + jnp.dot(
                    wb.astype(jnp.bfloat16), cached(b, 1), preferred_element_type=jnp.float32)
                top = new
            att[p, hd, :, pl.ds(j * HD, HD)] = (summed / total).astype(jnp.bfloat16)
        att_copy(p, hd, 1, x_peer).start()
        att_copy(p, hd, 0, core_peer).start()

    def relay(p):
        att_copy(p, x_peer, 2, core_peer).wait_recv()
        att_copy(p, x_peer, 2, core_peer).start()

    def project(p):
        other = (core_peer + 2) % n_head
        att_copy(p, core_peer, 0, core_peer).wait_recv()
        att_copy(p, other, 0, core_peer).wait_recv()
        for c in w_copies[p]:
            c.wait()
        rows_in = jnp.concatenate([att[p, i] for i in range(n_head)], axis=1)
        tile = 512
        for n in range(0, acc.shape[1], tile):
            part = jnp.dot(rows_in, w[p, :, n:n + tile], preferred_element_type=jnp.float32)
            if p > 0:
                part = part + acc[:, n:n + tile]
            if p < pieces - 1:
                acc[:, n:n + tile] = part
            else:
                row = gate[pl.ds(level_ref[0], 1), n:n + tile]
                mixed_ref[:, n:n + tile] = (part * row).astype(jnp.bfloat16)

    def convolve(first, number):
        at = [ext[pix + first - k * (pix // 2): pix + first - k * (pix // 2) + number, :] for k in range(3)]
        total = jnp.dot(at[0], cw[0], preferred_element_type=jnp.float32)
        total += jnp.dot(at[1], cw[1], preferred_element_type=jnp.float32)
        total += jnp.dot(at[2], cw[2], preferred_element_type=jnp.float32)
        dec_ref[first:first + number, :] = total.astype(jnp.bfloat16)

    halo = pltpu.make_async_remote_copy(
        ext.at[pl.ds(rows, pix)], ext.at[pl.ds(0, pix)], halo_send, halo_recv,
        device_id={"group": g + 1, "head": hd}, device_id_type=MESH)

    for p in range(min(ahead, pieces)):
        own_sends(p)
    for p in crossing:
        loaded(p)
        send_y(p, g).start()

    w_copies = []
    for p in range(pieces):
        w_copies.append([
            pltpu.make_async_copy(
                w_hbm.at[pl.ds((i * heads_local + p * per) * HD, wide)],
                w.at[p, pl.ds(i * wide, wide)], w_load.at[p, i])
            for i in range(n_head)])
        for c in w_copies[-1]:
            c.start()
    gate_copy.start()

    position = lax.broadcasted_iota(jnp.int32, (1, groups * krows), 1)
    owner, offset = position // krows, position % krows
    limit = jnp.zeros((1, groups * krows), jnp.int32)
    for j in range(groups):
        limit = jnp.where(owner == j, valid_ref[j], limit)
    usable = (owner < finished_ref[g]) & (offset < limit)
    bias[...] = jnp.where(usable, 0.0, NEGATIVE)

    @pl.when(g == 0)
    def _():
        ext[0:pix, :] = jnp.zeros((pix, ext.shape[1]), ext.dtype)

    lat_copy.wait()
    cw_copy.wait()
    convolve(pix, rows - pix)
    q_copy.wait()
    kn_copy.wait()
    vn_copy.wait()

    for k in range(pieces + skew * last):
        forward(k)
        if ahead <= k - skew + ahead < pieces:
            own_sends(k - skew + ahead)
        p = k - skew * last
        if p == pieces - 1:
            @pl.when(g < groups - 1)
            def _():
                halo.start()
        if p >= 1:
            relay(p - 1)
        if p >= 0:
            attend(p)
        if p >= 2:
            project(p - 2)

    gate_copy.wait()
    if pieces >= 2:
        project(pieces - 2)

    relay(pieces - 1)

    @pl.when(g > 0)
    def _():
        halo.wait_recv()

    convolve(0, pix)
    project(pieces - 1)

    @pl.when(g < groups - 1)
    def _():
        halo.wait_send()

    for p in range(pieces):
        finish_sends(p)
        att_copy(p, hd, 1, x_peer).wait_send()
        att_copy(p, hd, 0, core_peer).wait_send()
        att_copy(p, x_peer, 2, core_peer).wait_send()


def hand_over_kernel(mixed, decoded, mixed_out, decoded_out, sems):
    copies = [
        pltpu.make_async_copy(mixed, mixed_out, sems.at[0]),
        pltpu.make_async_copy(decoded, decoded_out, sems.at[1]),
    ]
    for c in copies:
        c.start()
    for c in copies:
        c.wait()


def hand_over(mixed, decoded):
    anywhere = pl.BlockSpec(memory_space=pl.ANY)
    vmem = pl.BlockSpec(memory_space=pltpu.VMEM)
    return pl.pallas_call(
        hand_over_kernel,
        out_shape=(
            jax.ShapeDtypeStruct(mixed.shape, mixed.dtype),
            jax.ShapeDtypeStruct(decoded.shape, decoded.dtype),
        ),
        in_specs=[vmem, vmem],
        out_specs=(anywhere, anywhere),
        scratch_shapes=[pltpu.SemaphoreType.DMA((2,))],
        name="hand_over",
    )(mixed, decoded)


def shards(
    groups, n_head,
    queries, keys_new, values_new, cache_keys, cache_values,
    valid_rows, finished, levels, gate_table, out_weight, latents, conv_weight,
):
    qrows, width = queries.shape
    krows = cache_keys.shape[0]
    heads_local = width // HD
    features = out_weight.shape[1]
    frames, pixels, channels = latents.shape
    pieces = heads_local if groups <= 8 else 1
    reach = min(1, groups // 2 - 1)
    per = heads_local // pieces
    crossing = ()
    cfg = (groups, pieces, per, 3, 2, reach, crossing)
    lines = groups // 2
    bf16, f32 = jnp.bfloat16, jnp.float32
    dma = pltpu.SemaphoreType.DMA
    hbm = pl.BlockSpec(memory_space=pl.ANY)
    smem = pl.BlockSpec(memory_space=pltpu.SMEM)
    vmem = pl.BlockSpec(memory_space=pltpu.VMEM)
    mixed, decoded = pl.pallas_call(
        functools.partial(kernel, cfg),
        out_shape=(
            jax.ShapeDtypeStruct((qrows, features), bf16),
            jax.ShapeDtypeStruct((frames * pixels, channels), bf16),
        ),
        in_specs=[hbm] * 5 + [smem] * 3 + [hbm] * 4,
        out_specs=(vmem, vmem),
        scratch_shapes=[
            pltpu.VMEM((pieces, groups, per, 2, krows, HD), bf16),
            pltpu.VMEM((qrows, width), bf16),
            pltpu.VMEM((qrows, width), bf16),
            pltpu.VMEM((qrows, width), bf16),
            pltpu.VMEM((pieces, n_head, qrows, per * HD), bf16),
            pltpu.VMEM((pieces, n_head * per * HD, features), bf16),
            pltpu.VMEM(gate_table.shape, f32),
            pltpu.VMEM(((frames + 2) * pixels, channels), bf16),
            pltpu.VMEM(conv_weight.shape, bf16),
            pltpu.VMEM((qrows, features), f32),
            pltpu.VMEM((1, groups * krows), f32),
            dma((2 * heads_local,)),
            dma((pieces, n_head)),
            dma((6,)),
            dma((pieces, groups)),
            dma((pieces, groups, reach)),
            dma((pieces, groups, reach)),
            dma((pieces, lines)),
            dma((pieces, n_head)),
            dma((pieces, 3)),
            dma,
            dma,
        ],
        compiler_params=pltpu.CompilerParams(
            collective_id=0, has_side_effects=True, vmem_limit_bytes=56 * 2**20),
        name="video_attention",
    )(
        queries, keys_new, values_new, cache_keys, cache_values,
        valid_rows, finished, levels, gate_table, out_weight,
        latents.reshape(frames * pixels, channels), conv_weight,
    )
    mixed, decoded = hand_over(mixed, decoded)
    return mixed, decoded.reshape(frames, pixels, channels)


def solution(mesh):
    in_specs = (
        P("group", "head"),
        P("group", "head"),
        P("group", "head"),
        P("group", "head"),
        P("group", "head"),
        P(),
        P(),
        P("group"),
        P(None, "head"),
        P(None, "head"),
        P("group", "head", None),
        P(),
    )
    out_specs = (P("group", "head"), P("group", "head", None))
    body = functools.partial(shards, mesh.shape["group"], mesh.shape["head"])
    return jax.shard_map(body, mesh=mesh, in_specs=in_specs, out_specs=out_specs, check_vma=False)
```
